32 devices in a mesh: beam: 2 (over y), freq: 8 (over z, x), tm: 2 (over core).
Axes of the slice: x: 2, y: 2, z: 4, core: 2. Of those that a mesh axis runs over, the one named last changes fastest.
Arguments:
- spectra: float32 [256, 16384], P(('beam', 'freq'), 'tm'), parts along dimension 0, may hold values from -250 to 250
- local_delays: int32 [4, 3, 128], P(None, None, 'freq'), may hold values from 0 to 8, as said below
- merge_delays: int32 [3, 3, 128], P(None, None, 'freq'), may hold values from 0 to 64, as said below
- widths: int32 [16], replicated, may hold values from 1 to 32, as said below
Outputs:
- detections: float32 [256, 16384], P(('beam', 'freq'), 'tm'), parts along dimension 0
The draws below stay inside these ranges and needn't reach their ends.
There are 2 independent parts, one for each index of `beam`. The reference program is written for one: setup_inputs(seed, part) draws one part's arguments, and reference() takes and returns one part's arrays. A program takes and returns all parts, laid end to end along the dimension named above; an argument that names none is the same for every part. Nothing has to cross between parts.
Inputs may be any that keep to these rules, and one draw needn't show every extreme that they name: `local_delays`: entries [s, 0, r] and [s, 1, r] lie in 0 to 2**s - 1, entry [s, 2, r] in 0 to 2**s, and [s, 2, 0] equals 2**s. `merge_delays`: entries [j, 0, r] and [j, 1, r] lie in 0 to 15, entry [j, 2, r] in 0 to 16 * 2**j, and [j, 2, 0] equals 16 * 2**j. 16 distinct widths, one of them 32.
All inputs are finite; a program needn't handle non-finite values.
Results may differ from the reference program's by a relative error of at most 0.00002.
Values sent between devices are 32-bit elements; how exact they have to be, the bound alone decides.
No kernel may reach another device: no remote copies, remote signals or barrier semaphores. Data moves between devices by JAX's collectives and lax.ppermute only.
A program may use at most 64 MiB of HBM per device.

```python
import math
import jax
import jax.numpy as jnp
from jax import lax

CH_DEV = 16
LLEVELS = 4
BLEVELS = 3
CHANNELS = 128
TIMES = 16384
WMAX = 32
NWIDTH = 16


def draw_spectra(key, part):
    subkeys = jax.random.split(key, 3)
    fraction = jnp.arange(TIMES, dtype=jnp.float32) / TIMES
    noise_part = jnp.clip(jax.random.normal(subkeys[0], (CHANNELS, TIMES), jnp.float32), -5.0, 5.0)
    channel_gain = jnp.exp(jax.random.uniform(subkeys[1], (CHANNELS, 1), jnp.float32, 0.0, math.log(10.0)))
    baseline = jax.random.uniform(subkeys[2], (CHANNELS, 1), jnp.float32, -2.0, 2.0)
    return channel_gain * (noise_part * (0.5 + fraction) + baseline * 3.0 * fraction)


def draw_local_delays(key, part):
    subkeys = jax.random.split(key, 3)
    level_size = (2 ** jnp.arange(LLEVELS, dtype=jnp.int32))[:, None]
    low_pick = jax.random.randint(subkeys[0], (LLEVELS, CHANNELS), 0, level_size)
    high_pick = jax.random.randint(subkeys[1], (LLEVELS, CHANNELS), 0, level_size)
    lag_table = jax.random.randint(subkeys[2], (LLEVELS, CHANNELS), 0, level_size + 1)
    lag_table = lag_table.at[:, 0].set(level_size[:, 0])
    return jnp.stack([low_pick, high_pick, lag_table], axis=1).astype(jnp.int32)


def draw_merge_delays(key, part):
    subkeys = jax.random.split(key, 3)
    level_size = (CH_DEV * 2 ** jnp.arange(BLEVELS, dtype=jnp.int32))[:, None]
    low_pick = jax.random.randint(subkeys[0], (BLEVELS, CHANNELS), 0, CH_DEV)
    high_pick = jax.random.randint(subkeys[1], (BLEVELS, CHANNELS), 0, CH_DEV)
    lag_table = jax.random.randint(subkeys[2], (BLEVELS, CHANNELS), 0, level_size + 1)
    lag_table = lag_table.at[:, 0].set(level_size[:, 0])
    return jnp.stack([low_pick, high_pick, lag_table], axis=1).astype(jnp.int32)


def draw_widths(key, part):
    shuffled = jax.random.permutation(key, WMAX - 1) + 1
    return jnp.concatenate([shuffled[:NWIDTH - 1], jnp.array([WMAX])]).astype(jnp.int32)


def setup_inputs(seed: int = 0, part: int = 0) -> dict:
    splits = jax.random.split(jax.random.key(seed), 5)
    part_keys = jax.random.split(jax.random.fold_in(splits[4], part), 5)
    return {
        "spectra": draw_spectra(jax.random.fold_in(jax.random.fold_in(splits[4], part), 71), part),
        "local_delays": draw_local_delays(jax.random.fold_in(splits[4], 71), part),
        "merge_delays": draw_merge_delays(jax.random.fold_in(splits[4], 71), part),
        "widths": draw_widths(jax.random.fold_in(splits[4], 71), part),
    }


EPSILON = 1e-05

def shift_rows(signal, delays, length):
    return jax.vmap(lambda one_row, one_lag: lax.dynamic_slice_in_dim(one_row, one_lag, length))(signal, delays)

def reference(spectra, local_delays, merge_delays, widths):
    average = lax.optimization_barrier(jnp.mean(spectra, axis=1, keepdims=True))
    centered = spectra - average
    variance = lax.optimization_barrier(jnp.mean(centered * centered, axis=1, keepdims=True))
    series = centered / jnp.sqrt(variance + EPSILON)
    row_ids = jnp.arange(CHANNELS, dtype=jnp.int32)
    for level_num in range(LLEVELS):
        level_size = 2 ** level_num
        base_row = row_ids // (2 * level_size) * (2 * level_size)
        low_rows = series[base_row + local_delays[level_num, 0]]
        high_rows = jnp.pad(series[base_row + level_size + local_delays[level_num, 1]], ((0, 0), (0, level_size)))
        series = low_rows + shift_rows(high_rows, local_delays[level_num, 2], TIMES)
    device_ids = row_ids // CH_DEV
    for level_num in range(BLEVELS):
        stride = 2 ** level_num
        low_device = device_ids - device_ids // stride % 2 * stride
        low_rows = series[low_device * CH_DEV + merge_delays[level_num, 0]]
        high_rows = series[(low_device + stride) * CH_DEV + merge_delays[level_num, 1]]
        high_rows = jnp.pad(high_rows, ((0, 0), (0, CH_DEV * stride)))
        series = low_rows + shift_rows(high_rows, merge_delays[level_num, 2], TIMES)
    extended = jnp.pad(series, ((0, 0), (0, WMAX - 1)))
    running = jnp.zeros((CHANNELS, TIMES), jnp.float32)
    strongest = jnp.full((CHANNELS, TIMES), -jnp.inf, jnp.float32)
    for offset in range(WMAX):
        running = running + extended[:, offset:offset + TIMES]
        chosen = jnp.any(widths == offset + 1)
        strongest = jnp.where(chosen, jnp.maximum(strongest, running * (1.0 / math.sqrt(offset + 1))), strongest)
    return strongest * (1.0 / math.sqrt(CHANNELS))
```

```python
import functools
import math

import jax
import jax.numpy as jnp
from jax import lax
from jax.experimental import pallas as pl
from jax.experimental.pallas import tpu as pltpu
from jax.sharding import PartitionSpec as P

WMAX = 32
LANES = 128
EPSILON = 1e-05
SHARES = (2, 3, 3)


def up(value, by):
    return -(-value // by) * by


def swap(value, axis, mask):
    pairs = [(source, source ^ mask) for source in range(lax.axis_size(axis))]
    return lax.ppermute(value, axis, pairs)


def shifted_tile(ref, base, delay, wide, lane):
    if wide:
        base = base + delay // LANES
        delay = delay % LANES
    here = ref[pl.ds(base, 8), :]
    after = ref[pl.ds(base + 1, 8), :]
    return pltpu.roll(jnp.where(lane >= delay, here, after), (LANES - delay) % LANES, 1)


def lanes():
    return lax.broadcasted_iota(jnp.int32, (8, LANES), 1)


class Plan:
    def __init__(self, channels, block_len, freq_count, tm_count):
        self.channels = channels
        self.rows = block_len // LANES
        self.freq_count = freq_count
        self.tm_count = tm_count
        self.local_levels = channels.bit_length() - 1
        self.levels = freq_count.bit_length() - 1
        tiles = self.rows // 8
        total = sum(SHARES)
        ends = [tiles - tiles * sum(SHARES[:i]) // total for i in range(len(SHARES) + 1)]
        self.chunks = [(8 * ends[i + 1], 8 * ends[i]) for i in range(len(SHARES))]
        reach = WMAX - 1
        need = [reach]
        for level in reversed(range(self.levels)):
            reach += channels * 2**level
            need.append(reach)
        self.ext = [-(-r // LANES) for r in reversed(need)]
        self.lead = -(-(reach + channels - 1) // LANES)

    def count(self, c):
        return self.chunks[c][1] - self.chunks[c][0]

    def message_rows(self, c, level):
        return self.channels * (self.count(c) + (self.ext[level] if c == 0 else 0))


def stats_kernel(plan, x_ref, widths_ref, msg_ref, caps_ref):
    ch, rows = plan.channels, plan.rows
    for group in range(ch // 8):
        base = group * rows * 8
        parts = [x_ref[pl.ds(base + 8 * i, 8), :] for i in range(8)]
        for i in range(8, rows):
            parts[i % 8] = parts[i % 8] + x_ref[pl.ds(base + 8 * i, 8), :]
        while len(parts) > 1:
            parts = [a + b for a, b in zip(parts[::2], parts[1::2])]
        mean = jnp.sum(parts[0], axis=1, keepdims=True) * (1.0 / (rows * LANES))
        mean = jnp.broadcast_to(mean, (8, LANES))
        parts = [jnp.zeros((8, LANES), jnp.float32) for _ in range(8)]
        for i in range(rows):
            off = x_ref[pl.ds(base + 8 * i, 8), :] - mean
            parts[i % 8] = parts[i % 8] + off * off
        while len(parts) > 1:
            parts = [a + b for a, b in zip(parts[::2], parts[1::2])]
        spread = jnp.sum(parts[0], axis=1, keepdims=True)
        msg_ref[pl.ds(8 * group, 8), :] = mean
        msg_ref[pl.ds(ch + 8 * group, 8), :] = jnp.broadcast_to(spread, (8, LANES))
        for i in range(plan.lead):
            msg_ref[pl.ds(2 * ch + (group * plan.lead + i) * 8, 8), :] = x_ref[pl.ds(base + 8 * i, 8), :]
    width = lax.broadcasted_iota(jnp.int32, (WMAX, LANES), 0) + 1
    caps = jnp.full((WMAX, LANES), -jnp.inf, jnp.float32)
    for k in range(widths_ref.shape[0]):
        caps = jnp.where(width == widths_ref[k], jnp.inf, caps)
    caps_ref[...] = caps


def local_kernel(plan, stride, x_ref, mine_ref, other_ref, delays_ref, *rest):
    outs, (stat, first, second) = rest[: len(plan.chunks)], rest[len(plan.chunks) :]
    ch, rows, lead = plan.channels, plan.rows, plan.lead
    half = rows * LANES
    mean_a, mean_b = mine_ref[pl.ds(0, ch), :], other_ref[pl.ds(0, ch), :]
    gap = mean_a - mean_b
    spread = mine_ref[pl.ds(ch, ch), :] + other_ref[pl.ds(ch, ch), :] + gap * gap * (half / 2.0)
    stat[pl.ds(0, ch), :] = (mean_a + mean_b) * 0.5
    stat[pl.ds(ch, ch), :] = 1.0 / jnp.sqrt(spread * (1.0 / (2 * half)) + EPSILON)
    last = lax.axis_index("tm") == plan.tm_count - 1
    keep = jnp.where(last, 0.0, 1.0).astype(jnp.float32)

    for r in range(ch):
        group, s = r // 8, r % 8
        mean = jnp.broadcast_to(stat[pl.ds(r, 1), :], (8, LANES))
        gain = jnp.broadcast_to(stat[pl.ds(ch + r, 1), :], (8, LANES))
        for k in range(rows // 8):
            tile = x_ref[pl.ds(group * rows * 8 + 64 * k + s, 8, stride=8), :]
            first[pl.ds(r * stride + 8 * k, 8), :] = (tile - mean) * gain
        for i in range(lead):
            row = other_ref[pl.ds(2 * ch + (group * lead + i) * 8 + s, 1), :]
            first[pl.ds(r * stride + rows + i, 1), :] = (row - mean[:1]) * (gain[:1] * keep)

    lane = lanes()
    source, target = first, second
    for level in range(plan.local_levels):
        size = 2**level
        final = level == plan.local_levels - 1
        tiles = (rows + up(lead, 8)) // 8
        for r in range(ch):
            base = r // (2 * size) * (2 * size)
            low = (base + delays_ref[level, 0, r]) * stride
            high = (base + size + delays_ref[level, 1, r]) * stride
            delay = delays_ref[level, 2, r]
            for k in range(tiles):
                tile = source[pl.ds(pl.multiple_of(low + 8 * k, 8), 8), :] + shifted_tile(
                    source, high + 8 * k, delay, False, lane
                )
                if not final:
                    target[pl.ds(r * stride + 8 * k, 8), :] = tile
                else:
                    put(plan, outs, 0, r, k, tile)
        source, target = target, source


def put(plan, outs, level, r, k, tile):
    for c, (start, stop) in enumerate(plan.chunks):
        if start <= 8 * k < stop:
            outs[c][pl.ds(r * (stop - start) + 8 * k - start, 8), :] = tile
    for i in range(8):
        past = 8 * k + i - plan.rows
        if 0 <= past < plan.ext[level]:
            at = plan.channels * plan.count(0) + past * plan.channels + r
            outs[0][pl.ds(at, 1), :] = tile[i : i + 1]


def gather_rows(plan, c, level, stride, both, own_ref, own_next, got_ref, got_next):
    ch, n = plan.channels, plan.count(c)
    span = ch * 2**level
    for side, (ref, following) in enumerate(((own_ref, own_next), (got_ref, got_next))):
        for r in range(ch):
            at = (side * ch + r) * stride
            for k in range(n // 8):
                both[pl.ds(at + 8 * k, 8), :] = ref[pl.ds(r * n + 8 * k, 8), :]
            if c == 0:
                for i in range(plan.ext[level]):
                    both[pl.ds(at + n + i, 1), :] = ref[pl.ds(ch * n + i * ch + r, 1), :]
            else:
                m = plan.count(c - 1)
                for k in range(up(span // LANES + 1, 8) // 8):
                    both[pl.ds(at + n + 8 * k, 8), :] = following[pl.ds(r * m + 8 * k, 8), :]


def merged_tile(plan, level, stride, both, delays_ref, upper, r, k, lane):
    ch = plan.channels
    low = (jnp.where(upper, ch, 0) + delays_ref[level, 0, r]) * stride + 8 * k
    high = (jnp.where(upper, 0, ch) + delays_ref[level, 1, r]) * stride + 8 * k
    wide = ch * 2**level >= LANES
    return both[pl.ds(pl.multiple_of(low, 8), 8), :] + shifted_tile(
        both, high, delays_ref[level, 2, r], wide, lane
    )


def merge_kernel(plan, c, level, stride, *refs):
    if c == 0:
        own_ref, got_ref, delays_ref, out_ref, both = refs
        own_next = got_next = None
    else:
        own_ref, own_next, got_ref, got_next, delays_ref, out_ref, both = refs
    n = plan.count(c)
    gather_rows(plan, c, level, stride, both, own_ref, own_next, got_ref, got_next)
    upper = lax.axis_index("freq") // 2**level % 2 == 1
    lane = lanes()
    rows = n + (up(plan.ext[level + 1], 8) if c == 0 else 0)
    outs = [None] * len(plan.chunks)
    outs[c] = out_ref
    for r in range(plan.channels):
        for k in range(rows // 8):
            tile = merged_tile(plan, level, stride, both, delays_ref, upper, r, k, lane)
            put(plan, outs, level + 1, r, k + plan.chunks[c][0] // 8, tile)


def final_kernel(plan, c, stride, *refs):
    level = plan.levels - 1
    ch, n = plan.channels, plan.count(c)
    if c == 0:
        own_ref, got_ref, delays_ref, caps_ref, out_ref, head_ref, both, series, box, sem = refs
        own_next = got_next = None
    else:
        (own_ref, own_next, got_ref, got_next, after_ref, delays_ref, caps_ref, _, out_ref, head_ref,
         both, series, box, sem) = refs
    gather_rows(plan, c, level, stride, both, own_ref, own_next, got_ref, got_next)
    upper = lax.axis_index("freq") // 2**level % 2 == 1
    lane = lanes()
    tiles = n // 8
    scale = 1.0 / math.sqrt(ch * plan.freq_count)
    pitch = n + 8
    for r in range(ch):
        for k in range(tiles + (1 if c == 0 else 0)):
            tile = merged_tile(plan, level, stride, both, delays_ref, upper, r, k, lane)
            series[pl.ds(r * pitch + 8 * k, 8), :] = tile
            if k == 0:
                head_ref[pl.ds(r, 1), :] = tile[:1]
        if c > 0:
            series[pl.ds(r * pitch + n, 1), :] = after_ref[pl.ds(r, 1), :]

    def one_row(r, carry):
        at = pl.multiple_of(r * pitch, 8)
        here = [series[pl.ds(at + 8 * k, 8), :] for k in range(tiles)]
        after = [series[pl.ds(at + 8 * k + 1, 8), :] for k in range(tiles)]
        running = here
        best = None
        for offset in range(WMAX):
            if offset:
                running = [
                    total + pltpu.roll(jnp.where(lane >= offset, a, b), LANES - offset, 1)
                    for total, a, b in zip(running, here, after)
                ]
            cap = jnp.broadcast_to(caps_ref[pl.ds(offset, 1), :], (8, LANES))
            factor = scale / math.sqrt(offset + 1)
            value = [jnp.minimum(total * factor, cap) for total in running]
            best = value if best is None else [jnp.maximum(a, b) for a, b in zip(best, value)]
        for k in range(tiles):
            box[pl.ds((r // 8) * (n * 8) + 64 * k + r % 8, 8, stride=8), :] = best[k]
        return carry

    lax.fori_loop(0, ch, one_row, 0)
    start = plan.chunks[c][0]
    copies = [
        pltpu.make_async_copy(
            box.at[pl.ds(group * n * 8, n * 8), :],
            out_ref.at[pl.ds((group * plan.rows + start) * 8, n * 8), :],
            sem.at[group],
        )
        for group in range(ch // 8)
    ]
    for copy in copies:
        copy.start()
    for copy in copies:
        copy.wait()


VMEM = pl.BlockSpec(memory_space=pltpu.VMEM)
SMEM = pl.BlockSpec(memory_space=pltpu.SMEM)
ANY = pl.BlockSpec(memory_space=pl.ANY)


def f32(*shape):
    return jax.ShapeDtypeStruct(shape, jnp.float32)


def call(kernel, ins, specs, outs, out_specs, scratch, ops, aliases=None):
    size = sum(math.prod(o.shape) for o in outs) * 4
    return pl.pallas_call(
        kernel,
        in_specs=specs,
        out_shape=outs,
        out_specs=out_specs,
        scratch_shapes=scratch,
        input_output_aliases=aliases or {},
        cost_estimate=pl.CostEstimate(flops=ops, bytes_accessed=3 * size, transcendentals=0),
        compiler_params=pltpu.CompilerParams(vmem_limit_bytes=24 * 2**20),
    )(*ins)


def per_device(plan, spectra, local_delays, merge_delays, widths):
    ch, rows = plan.channels, plan.rows
    chunks = range(len(plan.chunks))
    x = spectra.reshape(ch // 8, 8, rows, LANES).transpose(0, 2, 1, 3).reshape(ch * rows, LANES)
    msg, caps = call(
        functools.partial(stats_kernel, plan), (x, widths), [VMEM, SMEM],
        [f32(2 * ch + ch * plan.lead, LANES), f32(WMAX, LANES)], [VMEM, VMEM], [], 10**6,
    )
    other = swap(msg, "tm", 1)
    stride = rows + up(plan.lead, 8) + 8
    held = call(
        functools.partial(local_kernel, plan, stride), (x, msg, other, local_delays),
        [VMEM, VMEM, VMEM, SMEM], [f32(plan.message_rows(c, 0), LANES) for c in chunks],
        [VMEM for _ in chunks],
        [pltpu.VMEM((2 * ch, LANES), jnp.float32)] + [pltpu.VMEM((ch * stride, LANES), jnp.float32)] * 2,
        4 * 10**6,
    )
    for level in range(plan.levels):
        got = [swap(held[c], "freq", 2**level) for c in chunks]
        span = ch * 2**level
        made = []
        for c in chunks:
            n = plan.count(c)
            tail = max(up(plan.ext[level + 1], 8) if c == 0 else 0, 0) + span // LANES + 1
            tail = max(tail, plan.ext[level], up(span // LANES + 1, 8))
            stride = up(n + tail, 8)
            both = pltpu.VMEM((2 * ch * stride, LANES), jnp.float32)
            if c == 0:
                ins, specs = [held[0], got[0]], [VMEM] * 2
            else:
                ins, specs = [held[c], held[c - 1], got[c], got[c - 1]], [VMEM] * 4
            if level < plan.levels - 1:
                (out,) = call(
                    functools.partial(merge_kernel, plan, c, level, stride), (*ins, merge_delays),
                    [*specs, SMEM], [f32(plan.message_rows(c, level + 1), LANES)], [VMEM], [both],
                    8 * ch * n * LANES,
                )
                made.append(out)
                continue
            if c > 0:
                ins, specs = [*ins, head], [*specs, VMEM]
            ins, specs = [*ins, merge_delays, caps], [*specs, SMEM, VMEM]
            aliases = {}
            if c > 0:
                aliases = {len(ins): 0}
                ins, specs = [*ins, result], [*specs, ANY]
            result, head = call(
                functools.partial(final_kernel, plan, c, stride), ins, specs,
                [f32(ch * rows, LANES), f32(ch, LANES)], [ANY, VMEM],
                [both, pltpu.VMEM((ch * (n + 8), LANES), jnp.float32),
                 pltpu.VMEM((ch * n, LANES), jnp.float32), pltpu.SemaphoreType.DMA((ch // 8,))],
                200 * ch * n * LANES, aliases,
            )
        held = made
    return result.reshape(ch // 8, rows, 8, LANES).transpose(0, 2, 1, 3).reshape(ch, rows * LANES)


def solution(mesh):
    placed = (P(("beam", "freq"), "tm"), P(None, None, "freq"), P(None, None, "freq"), P())

    def whole(spectra, local_delays, merge_delays, widths):
        channels = spectra.shape[0] // (mesh.shape["beam"] * mesh.shape["freq"])
        block_len = spectra.shape[1] // mesh.shape["tm"]
        plan = Plan(channels, block_len, mesh.shape["freq"], mesh.shape["tm"])
        return jax.shard_map(
            functools.partial(per_device, plan), mesh=mesh, in_specs=placed,
            out_specs=P(("beam", "freq"), "tm"), check_vma=False,
        )(spectra, local_delays, merge_delays, widths)

    return whole
```

```python
import functools
import math

import jax
import jax.numpy as jnp
from jax import lax
from jax.experimental import pallas as pl
from jax.experimental.pallas import tpu as pltpu
from jax.sharding import PartitionSpec as P

WMAX = 32
LANES = 128
EPSILON = 1e-05
SHARES = (2, 3, 3)


def up(value, by):
    return -(-value // by) * by


def swap(value, axis, mask):
    pairs = [(source, source ^ mask) for source in range(lax.axis_size(axis))]
    return lax.ppermute(value, axis, pairs)


def shifted_tile(ref, base, delay, wide, lane):
    if wide:
        base = base + delay // LANES
        delay = delay % LANES
    here = ref[pl.ds(base, 8), :]
    after = ref[pl.ds(base + 1, 8), :]
    return pltpu.roll(jnp.where(lane >= delay, here, after), (LANES - delay) % LANES, 1)


def lanes():
    return lax.broadcasted_iota(jnp.int32, (8, LANES), 1)


class Plan:
    def __init__(self, channels, block_len, freq_count, tm_count):
        self.channels = channels
        self.rows = block_len // LANES
        self.freq_count = freq_count
        self.tm_count = tm_count
        self.local_levels = channels.bit_length() - 1
        self.levels = freq_count.bit_length() - 1
        tiles = self.rows // 8
        total = sum(SHARES)
        ends = [tiles - tiles * sum(SHARES[:i]) // total for i in range(len(SHARES) + 1)]
        self.chunks = [(8 * ends[i + 1], 8 * ends[i]) for i in range(len(SHARES))]
        reach = WMAX - 1
        need = [reach]
        for level in reversed(range(self.levels)):
            reach += channels * 2**level
            need.append(reach)
        self.ext = [-(-r // LANES) for r in reversed(need)]
        self.lead = -(-(reach + channels - 1) // LANES)

    def count(self, c):
        return self.chunks[c][1] - self.chunks[c][0]

    def message_rows(self, c, level):
        return self.channels * (self.count(c) + (self.ext[level] if c == 0 else 0))


def stats_kernel(plan, x_ref, msg_ref):
    ch, rows = plan.channels, plan.rows
    for group in range(ch // 8):
        base = group * rows * 8
        parts = [x_ref[pl.ds(base + 8 * i, 8), :] for i in range(8)]
        for i in range(8, rows):
            parts[i % 8] = parts[i % 8] + x_ref[pl.ds(base + 8 * i, 8), :]
        while len(parts) > 1:
            parts = [a + b for a, b in zip(parts[::2], parts[1::2])]
        mean = jnp.sum(parts[0], axis=1, keepdims=True) * (1.0 / (rows * LANES))
        mean = jnp.broadcast_to(mean, (8, LANES))
        parts = [jnp.zeros((8, LANES), jnp.float32) for _ in range(8)]
        for i in range(rows):
            off = x_ref[pl.ds(base + 8 * i, 8), :] - mean
            parts[i % 8] = parts[i % 8] + off * off
        while len(parts) > 1:
            parts = [a + b for a, b in zip(parts[::2], parts[1::2])]
        spread = jnp.sum(parts[0], axis=1, keepdims=True)
        msg_ref[pl.ds(8 * group, 8), :] = mean
        msg_ref[pl.ds(ch + 8 * group, 8), :] = jnp.broadcast_to(spread, (8, LANES))
        for i in range(plan.lead):
            msg_ref[pl.ds(2 * ch + (group * plan.lead + i) * 8, 8), :] = x_ref[pl.ds(base + 8 * i, 8), :]


def local_kernel(plan, stride, x_ref, mine_ref, other_ref, delays_ref, widths_ref, *rest):
    outs, (caps_ref, stat, first, second) = rest[: len(plan.chunks)], rest[len(plan.chunks) :]
    width = lax.broadcasted_iota(jnp.int32, (WMAX, LANES), 0) + 1
    caps = jnp.full((WMAX, LANES), -jnp.inf, jnp.float32)
    for k in range(widths_ref.shape[0]):
        caps = jnp.where(width == widths_ref[k], jnp.inf, caps)
    caps_ref[...] = caps
    ch, rows, lead = plan.channels, plan.rows, plan.lead
    half = rows * LANES
    mean_a, mean_b = mine_ref[pl.ds(0, ch), :], other_ref[pl.ds(0, ch), :]
    gap = mean_a - mean_b
    spread = mine_ref[pl.ds(ch, ch), :] + other_ref[pl.ds(ch, ch), :] + gap * gap * (half / 2.0)
    stat[pl.ds(0, ch), :] = (mean_a + mean_b) * 0.5
    stat[pl.ds(ch, ch), :] = 1.0 / jnp.sqrt(spread * (1.0 / (2 * half)) + EPSILON)
    last = lax.axis_index("tm") == plan.tm_count - 1
    keep = jnp.where(last, 0.0, 1.0).astype(jnp.float32)

    for r in range(ch):
        group, s = r // 8, r % 8
        mean = jnp.broadcast_to(stat[pl.ds(r, 1), :], (8, LANES))
        gain = jnp.broadcast_to(stat[pl.ds(ch + r, 1), :], (8, LANES))
        for k in range(rows // 8):
            tile = x_ref[pl.ds(group * rows * 8 + 64 * k + s, 8, stride=8), :]
            first[pl.ds(r * stride + 8 * k, 8), :] = (tile - mean) * gain
        for i in range(lead):
            row = other_ref[pl.ds(2 * ch + (group * lead + i) * 8 + s, 1), :]
            first[pl.ds(r * stride + rows + i, 1), :] = (row - mean[:1]) * (gain[:1] * keep)

    lane = lanes()
    source, target = first, second
    for level in range(plan.local_levels):
        size = 2**level
        final = level == plan.local_levels - 1
        tiles = (rows + up(lead, 8)) // 8
        for r in range(ch):
            base = r // (2 * size) * (2 * size)
            low = (base + delays_ref[level, 0, r]) * stride
            high = (base + size + delays_ref[level, 1, r]) * stride
            delay = delays_ref[level, 2, r]
            for k in range(tiles):
                tile = source[pl.ds(pl.multiple_of(low + 8 * k, 8), 8), :] + shifted_tile(
                    source, high + 8 * k, delay, False, lane
                )
                if not final:
                    target[pl.ds(r * stride + 8 * k, 8), :] = tile
                else:
                    put(plan, outs, 0, r, k, tile)
        source, target = target, source


def put(plan, outs, level, r, k, tile):
    for c, (start, stop) in enumerate(plan.chunks):
        if start <= 8 * k < stop:
            outs[c][pl.ds(r * (stop - start) + 8 * k - start, 8), :] = tile
    for i in range(8):
        past = 8 * k + i - plan.rows
        if 0 <= past < plan.ext[level]:
            at = plan.channels * plan.count(0) + past * plan.channels + r
            outs[0][pl.ds(at, 1), :] = tile[i : i + 1]


def gather_rows(plan, c, level, stride, both, own_ref, own_next, got_ref, got_next):
    ch, n = plan.channels, plan.count(c)
    span = ch * 2**level
    for side, (ref, following) in enumerate(((own_ref, own_next), (got_ref, got_next))):
        for r in range(ch):
            at = (side * ch + r) * stride
            for k in range(n // 8):
                both[pl.ds(at + 8 * k, 8), :] = ref[pl.ds(r * n + 8 * k, 8), :]
            if c == 0:
                for i in range(plan.ext[level]):
                    both[pl.ds(at + n + i, 1), :] = ref[pl.ds(ch * n + i * ch + r, 1), :]
            else:
                m = plan.count(c - 1)
                for k in range(up(span // LANES + 1, 8) // 8):
                    both[pl.ds(at + n + 8 * k, 8), :] = following[pl.ds(r * m + 8 * k, 8), :]


def merged_tile(plan, level, stride, both, delays_ref, upper, r, k, lane):
    ch = plan.channels
    low = (jnp.where(upper, ch, 0) + delays_ref[level, 0, r]) * stride + 8 * k
    high = (jnp.where(upper, 0, ch) + delays_ref[level, 1, r]) * stride + 8 * k
    wide = ch * 2**level >= LANES
    return both[pl.ds(pl.multiple_of(low, 8), 8), :] + shifted_tile(
        both, high, delays_ref[level, 2, r], wide, lane
    )


def merge_kernel(plan, c, level, stride, *refs):
    if c == 0:
        own_ref, got_ref, delays_ref, _, out_ref, both = refs
        own_next = got_next = None
    else:
        own_ref, own_next, got_ref, got_next, delays_ref, _, out_ref, both = refs
    n = plan.count(c)
    gather_rows(plan, c, level, stride, both, own_ref, own_next, got_ref, got_next)
    upper = lax.axis_index("freq") // 2**level % 2 == 1
    lane = lanes()
    rows = n + (up(plan.ext[level + 1], 8) if c == 0 else 0)
    outs = [None] * len(plan.chunks)
    outs[c] = out_ref
    for r in range(plan.channels):
        for k in range(rows // 8):
            tile = merged_tile(plan, level, stride, both, delays_ref, upper, r, k, lane)
            put(plan, outs, level + 1, r, k + plan.chunks[c][0] // 8, tile)


def boxcars(count, n, pitch, scale, series, caps_ref, box, lane):
    tiles = n // 8
    together = max(d for d in (1, 2, 4, 8) if d * tiles <= 8 or d == 1)

    def some_rows(step, carry):
        places = [(step * together + i, k) for i in range(together) for k in range(tiles)]
        here = [series[pl.ds(r * pitch + 8 * k, 8), :] for r, k in places]
        after = [series[pl.ds(r * pitch + 8 * k + 1, 8), :] for r, k in places]
        running = here
        best = None
        for offset in range(WMAX):
            if offset:
                running = [
                    total + pltpu.roll(jnp.where(lane >= offset, a, b), LANES - offset, 1)
                    for total, a, b in zip(running, here, after)
                ]
            cap = jnp.broadcast_to(caps_ref[pl.ds(offset, 1), :], (8, LANES))
            factor = scale / math.sqrt(offset + 1)
            value = [jnp.minimum(total * factor, cap) for total in running]
            best = value if best is None else [jnp.maximum(a, b) for a, b in zip(best, value)]
        for (r, k), tile in zip(places, best):
            box[pl.ds((r // 8) * (n * 8) + 64 * k + r % 8, 8, stride=8), :] = tile
        return carry

    lax.fori_loop(0, count // together, some_rows, 0)


def final_kernel(plan, c, stride, *refs):
    level = plan.levels - 1
    ch, n = plan.channels, plan.count(c)
    if c == 0:
        own_ref, got_ref, delays_ref, caps_ref, _, out_ref, head_ref, both, series, box, sem = refs
        own_next = got_next = None
    else:
        (own_ref, own_next, got_ref, got_next, after_ref, delays_ref, caps_ref, _, _, out_ref, head_ref,
         both, series, box, sem) = refs
    gather_rows(plan, c, level, stride, both, own_ref, own_next, got_ref, got_next)
    upper = lax.axis_index("freq") // 2**level % 2 == 1
    lane = lanes()
    tiles = n // 8
    scale = 1.0 / math.sqrt(ch * plan.freq_count)
    pitch = n + 8
    for r in range(ch):
        for k in range(tiles + (1 if c == 0 else 0)):
            tile = merged_tile(plan, level, stride, both, delays_ref, upper, r, k, lane)
            series[pl.ds(r * pitch + 8 * k, 8), :] = tile
            if k == 0:
                head_ref[pl.ds(r, 1), :] = tile[:1]
        if c > 0:
            series[pl.ds(r * pitch + n, 1), :] = after_ref[pl.ds(r, 1), :]

    boxcars(ch, n, pitch, scale, series, caps_ref, box, lane)
    start = plan.chunks[c][0]
    copies = [
        pltpu.make_async_copy(
            box.at[pl.ds(group * n * 8, n * 8), :],
            out_ref.at[pl.ds((group * plan.rows + start) * 8, n * 8), :],
            sem.at[group],
        )
        for group in range(ch // 8)
    ]
    for copy in copies:
        copy.start()
    for copy in copies:
        copy.wait()


VMEM = pl.BlockSpec(memory_space=pltpu.VMEM)
SMEM = pl.BlockSpec(memory_space=pltpu.SMEM)
ANY = pl.BlockSpec(memory_space=pl.ANY)


def f32(*shape):
    return jax.ShapeDtypeStruct(shape, jnp.float32)


def call(kernel, ins, specs, outs, out_specs, scratch, aliases=None):
    return pl.pallas_call(
        kernel,
        in_specs=specs,
        out_shape=outs,
        out_specs=out_specs,
        scratch_shapes=scratch,
        input_output_aliases=aliases or {},
        cost_estimate=pl.CostEstimate(flops=1, bytes_accessed=1, transcendentals=0),
        compiler_params=pltpu.CompilerParams(vmem_limit_bytes=24 * 2**20),
    )(*ins)


def per_device(plan, spectra, local_delays, merge_delays, widths):
    ch, rows = plan.channels, plan.rows
    chunks = range(len(plan.chunks))
    x = spectra.reshape(ch // 8, 8, rows, LANES).transpose(0, 2, 1, 3).reshape(ch * rows, LANES)
    (msg,) = call(
        functools.partial(stats_kernel, plan), (x,), [VMEM], [f32(2 * ch + ch * plan.lead, LANES)], [VMEM], [],
    )
    other = swap(msg, "tm", 1)
    stride = rows + up(plan.lead, 8) + 8
    *first, caps = call(
        functools.partial(local_kernel, plan, stride), (x, msg, other, local_delays, widths),
        [VMEM, VMEM, VMEM, SMEM, SMEM], [*(f32(plan.message_rows(c, 0), LANES) for c in chunks), f32(WMAX, LANES)],
        [VMEM for _ in range(len(chunks) + 1)],
        [pltpu.VMEM((2 * ch, LANES), jnp.float32)] + [pltpu.VMEM((ch * stride, LANES), jnp.float32)] * 2,
    )
    held, got = {}, {}
    for c in chunks:
        held[0, c] = first[c]
        got[0, c] = swap(first[c], "freq", 1)
    last, head, result = caps, None, None
    for wave in range(len(chunks) + plan.levels - 1):
        for level in range(plan.levels):
            c = wave - level
            if c not in chunks:
                continue
            n = plan.count(c)
            span = ch * 2**level
            ahead = span // LANES + 1
            tail = max((up(plan.ext[level + 1], 8) if c == 0 else 0) + ahead, plan.ext[level], up(ahead, 8))
            stride = up(n + tail, 8)
            both = pltpu.VMEM((2 * ch * stride, LANES), jnp.float32)
            near = [c] if c == 0 else [c, c - 1]
            ins = [group[level, i] for group in (held, got) for i in near]
            specs = [VMEM] * len(ins)
            if level < plan.levels - 1:
                (last,) = call(
                    functools.partial(merge_kernel, plan, c, level, stride), (*ins, merge_delays, last),
                    [*specs, SMEM, ANY], [f32(plan.message_rows(c, level + 1), LANES)], [VMEM], [both],
                )
                held[level + 1, c] = last
                got[level + 1, c] = swap(last, "freq", 2 ** (level + 1))
                continue
            if c > 0:
                ins, specs = [*ins, head], [*specs, VMEM]
            ins, specs = [*ins, merge_delays, caps, last], [*specs, SMEM, VMEM, ANY]
            aliases = {}
            if c > 0:
                aliases = {len(ins): 0}
                ins, specs = [*ins, result], [*specs, ANY]
            result, head = call(
                functools.partial(final_kernel, plan, c, stride), ins, specs,
                [f32(ch * rows, LANES), f32(ch, LANES)], [ANY, VMEM],
                [both, pltpu.VMEM((ch * (n + 8), LANES), jnp.float32),
                 pltpu.VMEM((ch * n, LANES), jnp.float32), pltpu.SemaphoreType.DMA((ch // 8,))], aliases,
            )
            last = head
    return result.reshape(ch // 8, rows, 8, LANES).transpose(0, 2, 1, 3).reshape(ch, rows * LANES)


def solution(mesh):
    placed = (P(("beam", "freq"), "tm"), P(None, None, "freq"), P(None, None, "freq"), P())

    def whole(spectra, local_delays, merge_delays, widths):
        channels = spectra.shape[0] // (mesh.shape["beam"] * mesh.shape["freq"])
        block_len = spectra.shape[1] // mesh.shape["tm"]
        plan = Plan(channels, block_len, mesh.shape["freq"], mesh.shape["tm"])
        return jax.shard_map(
            functools.partial(per_device, plan), mesh=mesh, in_specs=placed,
            out_specs=P(("beam", "freq"), "tm"), check_vma=False,
        )(spectra, local_delays, merge_delays, widths)

    return whole
```

```python
import functools
import math

import jax
import jax.numpy as jnp
from jax import lax
from jax.experimental import pallas as pl
from jax.experimental.pallas import tpu as pltpu
from jax.sharding import PartitionSpec as P

WMAX = 32
LANES = 128
EPSILON = 1e-05
SHARES = (2, 2, 2, 2)


def up(value, by):
    return -(-value // by) * by


def swap(value, axis, mask):
    pairs = [(source, source ^ mask) for source in range(lax.axis_size(axis))]
    return lax.ppermute(value, axis, pairs)


def shifted_tile(ref, base, delay, wide, lane):
    if wide:
        base = base + delay // LANES
        delay = delay % LANES
    here = ref[pl.ds(base, 8), :]
    after = ref[pl.ds(base + 1, 8), :]
    return pltpu.roll(jnp.where(lane >= delay, here, after), (LANES - delay) % LANES, 1)


def lanes():
    return lax.broadcasted_iota(jnp.int32, (8, LANES), 1)


STEP, WAIT = 1.5, 0.0


def turn(plan):
    return lambda job: (job[1] + STEP * job[0] + WAIT * (job[0] == plan.levels - 1), job[0])


class Plan:
    def __init__(self, channels, block_len, freq_count, tm_count):
        self.channels = channels
        self.rows = block_len // LANES
        self.freq_count = freq_count
        self.tm_count = tm_count
        self.local_levels = channels.bit_length() - 1
        self.levels = freq_count.bit_length() - 1
        tiles = self.rows // 8
        total = sum(SHARES)
        ends = [tiles - tiles * sum(SHARES[:i]) // total for i in range(len(SHARES) + 1)]
        self.chunks = [(8 * ends[i + 1], 8 * ends[i]) for i in range(len(SHARES))]
        reach = WMAX - 1
        need = [reach]
        for level in reversed(range(self.levels)):
            reach += channels * 2**level
            need.append(reach)
        self.ext = [-(-r // LANES) for r in reversed(need)]
        self.lead = -(-(reach + channels - 1) // LANES)

    def count(self, c):
        return self.chunks[c][1] - self.chunks[c][0]

    def message_rows(self, c, level):
        return self.channels * (self.count(c) + (self.ext[level] if c == 0 else 0))


def stats_kernel(plan, x_ref, msg_ref):
    ch, rows = plan.channels, plan.rows
    for group in range(ch // 8):
        base = group * rows * 8
        parts = [x_ref[pl.ds(base + 8 * i, 8), :] for i in range(8)]
        for i in range(8, rows):
            parts[i % 8] = parts[i % 8] + x_ref[pl.ds(base + 8 * i, 8), :]
        while len(parts) > 1:
            parts = [a + b for a, b in zip(parts[::2], parts[1::2])]
        mean = jnp.sum(parts[0], axis=1, keepdims=True) * (1.0 / (rows * LANES))
        mean = jnp.broadcast_to(mean, (8, LANES))
        parts = [jnp.zeros((8, LANES), jnp.float32) for _ in range(8)]
        for i in range(rows):
            off = x_ref[pl.ds(base + 8 * i, 8), :] - mean
            parts[i % 8] = parts[i % 8] + off * off
        while len(parts) > 1:
            parts = [a + b for a, b in zip(parts[::2], parts[1::2])]
        spread = jnp.sum(parts[0], axis=1, keepdims=True)
        msg_ref[pl.ds(8 * group, 8), :] = mean
        msg_ref[pl.ds(ch + 8 * group, 8), :] = jnp.broadcast_to(spread, (8, LANES))
        for i in range(plan.lead):
            msg_ref[pl.ds(2 * ch + (group * plan.lead + i) * 8, 8), :] = x_ref[pl.ds(base + 8 * i, 8), :]


def local_kernel(plan, stride, x_ref, mine_ref, other_ref, delays_ref, widths_ref, *rest):
    outs, (caps_ref, stat, first, second) = rest[: len(plan.chunks)], rest[len(plan.chunks) :]
    width = lax.broadcasted_iota(jnp.int32, (WMAX, LANES), 0) + 1
    caps = jnp.full((WMAX, LANES), -jnp.inf, jnp.float32)
    for k in range(widths_ref.shape[0]):
        caps = jnp.where(width == widths_ref[k], jnp.inf, caps)
    caps_ref[...] = caps
    ch, rows, lead = plan.channels, plan.rows, plan.lead
    half = rows * LANES
    mean_a, mean_b = mine_ref[pl.ds(0, ch), :], other_ref[pl.ds(0, ch), :]
    gap = mean_a - mean_b
    spread = mine_ref[pl.ds(ch, ch), :] + other_ref[pl.ds(ch, ch), :] + gap * gap * (half / 2.0)
    stat[pl.ds(0, ch), :] = (mean_a + mean_b) * 0.5
    stat[pl.ds(ch, ch), :] = 1.0 / jnp.sqrt(spread * (1.0 / (2 * half)) + EPSILON)
    last = lax.axis_index("tm") == plan.tm_count - 1
    keep = jnp.where(last, 0.0, 1.0).astype(jnp.float32)

    for r in range(ch):
        group, s = r // 8, r % 8
        mean = jnp.broadcast_to(stat[pl.ds(r, 1), :], (8, LANES))
        gain = jnp.broadcast_to(stat[pl.ds(ch + r, 1), :], (8, LANES))
        for k in range(rows // 8):
            tile = x_ref[pl.ds(group * rows * 8 + 64 * k + s, 8, stride=8), :]
            first[pl.ds(r * stride + 8 * k, 8), :] = (tile - mean) * gain
        for i in range(lead):
            row = other_ref[pl.ds(2 * ch + (group * lead + i) * 8 + s, 1), :]
            first[pl.ds(r * stride + rows + i, 1), :] = (row - mean[:1]) * (gain[:1] * keep)

    lane = lanes()
    source, target = first, second
    for level in range(plan.local_levels):
        size = 2**level
        final = level == plan.local_levels - 1
        tiles = (rows + up(lead, 8)) // 8
        jobs = table(delays_ref, level, ch)
        for r, (low, high, delay) in enumerate(jobs):
            base = r // (2 * size) * (2 * size)
            low = (base + low) * stride
            high = (base + size + high) * stride
            for k in range(tiles):
                tile = source[pl.ds(pl.multiple_of(low + 8 * k, 8), 8), :] + shifted_tile(
                    source, high + 8 * k, delay, False, lane
                )
                if not final:
                    target[pl.ds(r * stride + 8 * k, 8), :] = tile
                else:
                    put(plan, outs, 0, r, k, tile)
        source, target = target, source


def put(plan, outs, level, r, k, tile):
    for c, (start, stop) in enumerate(plan.chunks):
        if start <= 8 * k < stop:
            outs[c][pl.ds(r * (stop - start) + 8 * k - start, 8), :] = tile
    for i in range(8):
        past = 8 * k + i - plan.rows
        if 0 <= past < plan.ext[level]:
            at = plan.channels * plan.count(0) + past * plan.channels + r
            outs[0][pl.ds(at, 1), :] = tile[i : i + 1]


def gather_rows(plan, c, level, stride, both, own_ref, own_next, got_ref, got_next):
    ch, n = plan.channels, plan.count(c)
    span = ch * 2**level
    for side, (ref, following) in enumerate(((own_ref, own_next), (got_ref, got_next))):
        for r in range(ch):
            at = (side * ch + r) * stride
            for k in range(n // 8):
                both[pl.ds(at + 8 * k, 8), :] = ref[pl.ds(r * n + 8 * k, 8), :]
            if c == 0:
                for i in range(plan.ext[level]):
                    both[pl.ds(at + n + i, 1), :] = ref[pl.ds(ch * n + i * ch + r, 1), :]
            else:
                m = plan.count(c - 1)
                for k in range(up(span // LANES + 1, 8) // 8):
                    both[pl.ds(at + n + 8 * k, 8), :] = following[pl.ds(r * m + 8 * k, 8), :]


def table(delays_ref, level, count):
    return [tuple(delays_ref[level, i, r] for i in range(3)) for r in range(count)]


def merge_jobs(plan, level, stride, delays_ref):
    ch = plan.channels
    upper = lax.axis_index("freq") // 2**level % 2 == 1
    first, second = jnp.where(upper, ch, 0), jnp.where(upper, 0, ch)
    return [((first + a) * stride, (second + b) * stride, d) for a, b, d in table(delays_ref, level, ch)]


def merged_tile(plan, level, both, job, k, lane):
    low, high, delay = job
    wide = plan.channels * 2**level >= LANES
    return both[pl.ds(pl.multiple_of(low + 8 * k, 8), 8), :] + shifted_tile(
        both, high + 8 * k, delay, wide, lane
    )


def merge_kernel(plan, c, level, stride, *refs):
    if c == 0:
        own_ref, got_ref, delays_ref, _, out_ref, both = refs
        own_next = got_next = None
    else:
        own_ref, own_next, got_ref, got_next, delays_ref, _, out_ref, both = refs
    n = plan.count(c)
    jobs = merge_jobs(plan, level, stride, delays_ref)
    gather_rows(plan, c, level, stride, both, own_ref, own_next, got_ref, got_next)
    lane = lanes()
    rows = n + (up(plan.ext[level + 1], 8) if c == 0 else 0)
    outs = [None] * len(plan.chunks)
    outs[c] = out_ref
    for r in range(plan.channels):
        for k in range(rows // 8):
            tile = merged_tile(plan, level, both, jobs[r], k, lane)
            put(plan, outs, level + 1, r, k + plan.chunks[c][0] // 8, tile)


def boxcars(count, n, pitch, scale, series, caps_ref, box, lane):
    tiles = n // 8
    together = max(d for d in (1, 2, 4, 8) if d * tiles <= 8 or d == 1)

    def some_rows(step, carry):
        places = [(step * together + i, k) for i in range(together) for k in range(tiles)]
        here = [series[pl.ds(r * pitch + 8 * k, 8), :] for r, k in places]
        after = [series[pl.ds(r * pitch + 8 * k + 1, 8), :] for r, k in places]
        running = here
        best = None
        for offset in range(WMAX):
            if offset:
                running = [
                    total + pltpu.roll(jnp.where(lane >= offset, a, b), LANES - offset, 1)
                    for total, a, b in zip(running, here, after)
                ]
            cap = jnp.broadcast_to(caps_ref[pl.ds(offset, 1), :], (8, LANES))
            factor = scale / math.sqrt(offset + 1)
            value = [jnp.minimum(total * factor, cap) for total in running]
            best = value if best is None else [jnp.maximum(a, b) for a, b in zip(best, value)]
        for (r, k), tile in zip(places, best):
            box[pl.ds((r // 8) * (n * 8) + 64 * k + r % 8, 8, stride=8), :] = tile
        return carry

    lax.fori_loop(0, count // together, some_rows, 0)


def final_kernel(plan, c, stride, *refs):
    level = plan.levels - 1
    ch, n = plan.channels, plan.count(c)
    if c == 0:
        own_ref, got_ref, delays_ref, caps_ref, _, out_ref, head_ref, both, series, box, sem = refs
        own_next = got_next = None
    else:
        (own_ref, own_next, got_ref, got_next, after_ref, delays_ref, caps_ref, _, _, out_ref, head_ref,
         both, series, box, sem) = refs
    jobs = merge_jobs(plan, level, stride, delays_ref)
    gather_rows(plan, c, level, stride, both, own_ref, own_next, got_ref, got_next)
    lane = lanes()
    tiles = n // 8
    scale = 1.0 / math.sqrt(ch * plan.freq_count)
    pitch = n + 8
    for r in range(ch):
        for k in range(tiles + (1 if c == 0 else 0)):
            tile = merged_tile(plan, level, both, jobs[r], k, lane)
            series[pl.ds(r * pitch + 8 * k, 8), :] = tile
            if k == 0:
                head_ref[pl.ds(r, 1), :] = tile[:1]
        if c > 0:
            series[pl.ds(r * pitch + n, 1), :] = after_ref[pl.ds(r, 1), :]

    boxcars(ch, n, pitch, scale, series, caps_ref, box, lane)
    start = plan.chunks[c][0]
    copies = [
        pltpu.make_async_copy(
            box.at[pl.ds(group * n * 8, n * 8), :],
            out_ref.at[pl.ds((group * plan.rows + start) * 8, n * 8), :],
            sem.at[group],
        )
        for group in range(ch // 8)
    ]
    for copy in copies:
        copy.start()
    for copy in copies:
        copy.wait()


VMEM = pl.BlockSpec(memory_space=pltpu.VMEM)
SMEM = pl.BlockSpec(memory_space=pltpu.SMEM)
ANY = pl.BlockSpec(memory_space=pl.ANY)


def f32(*shape):
    return jax.ShapeDtypeStruct(shape, jnp.float32)


def call(kernel, ins, specs, outs, out_specs, scratch, aliases=None):
    return pl.pallas_call(
        kernel,
        in_specs=specs,
        out_shape=outs,
        out_specs=out_specs,
        scratch_shapes=scratch,
        input_output_aliases=aliases or {},
        cost_estimate=pl.CostEstimate(flops=1, bytes_accessed=1, transcendentals=0),
        compiler_params=pltpu.CompilerParams(vmem_limit_bytes=24 * 2**20),
    )(*ins)


def per_device(plan, spectra, local_delays, merge_delays, widths):
    ch, rows = plan.channels, plan.rows
    chunks = range(len(plan.chunks))
    x = spectra.reshape(ch // 8, 8, rows, LANES).transpose(0, 2, 1, 3).reshape(ch * rows, LANES)
    (msg,) = call(
        functools.partial(stats_kernel, plan), (x,), [VMEM], [f32(2 * ch + ch * plan.lead, LANES)], [VMEM], [],
    )
    other = swap(msg, "tm", 1)
    stride = rows + up(plan.lead, 8) + 8
    *first, caps = call(
        functools.partial(local_kernel, plan, stride), (x, msg, other, local_delays, widths),
        [VMEM, VMEM, VMEM, VMEM, VMEM], [*(f32(plan.message_rows(c, 0), LANES) for c in chunks), f32(WMAX, LANES)],
        [VMEM for _ in range(len(chunks) + 1)],
        [pltpu.VMEM((2 * ch, LANES), jnp.float32)] + [pltpu.VMEM((ch * stride, LANES), jnp.float32)] * 2,
    )
    held, got = {}, {}
    for c in chunks:
        held[0, c] = first[c]
        got[0, c] = swap(first[c], "freq", 1)
    last, head, result = caps, None, None
    for level, c in sorted(((level, c) for level in range(plan.levels) for c in chunks), key=turn(plan)):
        if True:
            n = plan.count(c)
            span = ch * 2**level
            ahead = span // LANES + 1
            tail = max((up(plan.ext[level + 1], 8) if c == 0 else 0) + ahead, plan.ext[level], up(ahead, 8))
            stride = up(n + tail, 8)
            both = pltpu.VMEM((2 * ch * stride, LANES), jnp.float32)
            near = [c] if c == 0 else [c, c - 1]
            ins = [group[level, i] for group in (held, got) for i in near]
            specs = [VMEM] * len(ins)
            if level < plan.levels - 1:
                (last,) = call(
                    functools.partial(merge_kernel, plan, c, level, stride), (*ins, merge_delays, last),
                    [*specs, VMEM, ANY], [f32(plan.message_rows(c, level + 1), LANES)], [VMEM], [both],
                )
                held[level + 1, c] = last
                got[level + 1, c] = swap(last, "freq", 2 ** (level + 1))
                continue
            if c > 0:
                ins, specs = [*ins, head], [*specs, VMEM]
            ins, specs = [*ins, merge_delays, caps, last], [*specs, VMEM, VMEM, ANY]
            aliases = {}
            if c > 0:
                aliases = {len(ins): 0}
                ins, specs = [*ins, result], [*specs, ANY]
            result, head = call(
                functools.partial(final_kernel, plan, c, stride), ins, specs,
                [f32(ch * rows, LANES), f32(ch, LANES)], [ANY, VMEM],
                [both, pltpu.VMEM((ch * (n + 8), LANES), jnp.float32),
                 pltpu.VMEM((ch * n, LANES), jnp.float32), pltpu.SemaphoreType.DMA((ch // 8,))], aliases,
            )
            last = head
    return result.reshape(ch // 8, rows, 8, LANES).transpose(0, 2, 1, 3).reshape(ch, rows * LANES)


def solution(mesh):
    placed = (P(("beam", "freq"), "tm"), P(None, None, "freq"), P(None, None, "freq"), P())

    def whole(spectra, local_delays, merge_delays, widths):
        channels = spectra.shape[0] // (mesh.shape["beam"] * mesh.shape["freq"])
        block_len = spectra.shape[1] // mesh.shape["tm"]
        plan = Plan(channels, block_len, mesh.shape["freq"], mesh.shape["tm"])
        return jax.shard_map(
            functools.partial(per_device, plan), mesh=mesh, in_specs=placed,
            out_specs=P(("beam", "freq"), "tm"), check_vma=False,
        )(spectra, local_delays, merge_delays, widths)

    return whole
```

```python
import functools
import math

import jax
import jax.numpy as jnp
from jax import lax
from jax.experimental import pallas as pl
from jax.experimental.pallas import tpu as pltpu
from jax.sharding import PartitionSpec as P

WMAX = 32
LANES = 128
EPSILON = 1e-05
SHARES = (2, 2, 2, 2)


def up(value, by):
    return -(-value // by) * by


def swap(value, axis, mask):
    pairs = [(source, source ^ mask) for source in range(lax.axis_size(axis))]
    return lax.ppermute(value, axis, pairs)


def shifted_tile(ref, base, delay, wide, lane):
    if wide:
        base = base + delay // LANES
        delay = delay % LANES
    here = ref[pl.ds(base, 8), :]
    after = ref[pl.ds(base + 1, 8), :]
    return pltpu.roll(jnp.where(lane >= delay, here, after), (LANES - delay) % LANES, 1)


def lanes():
    return lax.broadcasted_iota(jnp.int32, (8, LANES), 1)


STEP, WAIT = 1.5, 0.0


def turn(plan):
    return lambda job: (job[1] + STEP * job[0] + WAIT * (job[0] == plan.levels - 1), job[0])


class Plan:
    def __init__(self, channels, block_len, freq_count, tm_count):
        self.channels = channels
        self.rows = block_len // LANES
        self.freq_count = freq_count
        self.tm_count = tm_count
        self.local_levels = channels.bit_length() - 1
        self.levels = freq_count.bit_length() - 1
        tiles = self.rows // 8
        total = sum(SHARES)
        ends = [tiles - tiles * sum(SHARES[:i]) // total for i in range(len(SHARES) + 1)]
        self.chunks = [(8 * ends[i + 1], 8 * ends[i]) for i in range(len(SHARES))]
        reach = WMAX - 1
        need = [reach]
        for level in reversed(range(self.levels)):
            reach += channels * 2**level
            need.append(reach)
        self.ext = [-(-r // LANES) for r in reversed(need)]
        self.lead = -(-(reach + channels - 1) // LANES)

    def count(self, c):
        return self.chunks[c][1] - self.chunks[c][0]

    def message_rows(self, c, level):
        return self.channels * (self.count(c) + (self.ext[level] if c == 0 else 0))


def stats_kernel(plan, x_ref, msg_ref):
    ch, rows = plan.channels, plan.rows
    for group in range(ch // 8):
        base = group * rows * 8
        parts = [x_ref[pl.ds(base + 8 * i, 8), :] for i in range(8)]
        for i in range(8, rows):
            parts[i % 8] = parts[i % 8] + x_ref[pl.ds(base + 8 * i, 8), :]
        while len(parts) > 1:
            parts = [a + b for a, b in zip(parts[::2], parts[1::2])]
        mean = jnp.sum(parts[0], axis=1, keepdims=True) * (1.0 / (rows * LANES))
        mean = jnp.broadcast_to(mean, (8, LANES))
        parts = [jnp.zeros((8, LANES), jnp.float32) for _ in range(8)]
        for i in range(rows):
            off = x_ref[pl.ds(base + 8 * i, 8), :] - mean
            parts[i % 8] = parts[i % 8] + off * off
        while len(parts) > 1:
            parts = [a + b for a, b in zip(parts[::2], parts[1::2])]
        spread = jnp.sum(parts[0], axis=1, keepdims=True)
        msg_ref[pl.ds(8 * group, 8), :] = mean
        msg_ref[pl.ds(ch + 8 * group, 8), :] = jnp.broadcast_to(spread, (8, LANES))
        for i in range(plan.lead):
            msg_ref[pl.ds(2 * ch + (group * plan.lead + i) * 8, 8), :] = x_ref[pl.ds(base + 8 * i, 8), :]


def local_kernel(plan, begin, end, stride, x_ref, mine_ref, other_ref, delays_ref, widths_ref, *rest):
    ch, rows, lead = plan.channels, plan.rows, plan.lead
    ending = end == rows
    here = [c for c, (start, _) in enumerate(plan.chunks) if begin <= start < end]
    rest = rest if ending else rest[1:]
    outs = dict(zip(here, rest))
    stat, first, second = rest[-3:]
    half = rows * LANES
    if not ending:
        width = lax.broadcasted_iota(jnp.int32, (WMAX, LANES), 0) + 1
        caps = jnp.full((WMAX, LANES), -jnp.inf, jnp.float32)
        for k in range(widths_ref.shape[0]):
            caps = jnp.where(width == widths_ref[k], jnp.inf, caps)
        rest[len(here)][...] = caps
    mean_a, mean_b = mine_ref[pl.ds(0, ch), :], other_ref[pl.ds(0, ch), :]
    gap = mean_a - mean_b
    spread = mine_ref[pl.ds(ch, ch), :] + other_ref[pl.ds(ch, ch), :] + gap * gap * (half / 2.0)
    stat[pl.ds(0, ch), :] = (mean_a + mean_b) * 0.5
    stat[pl.ds(ch, ch), :] = 1.0 / jnp.sqrt(spread * (1.0 / (2 * half)) + EPSILON)
    last = lax.axis_index("tm") == plan.tm_count - 1
    keep = jnp.where(last, 0.0, 1.0).astype(jnp.float32)

    for r in range(ch):
        group, s = r // 8, r % 8
        mean = jnp.broadcast_to(stat[pl.ds(r, 1), :], (8, LANES))
        gain = jnp.broadcast_to(stat[pl.ds(ch + r, 1), :], (8, LANES))
        for k in range(begin // 8, min(end + 8, rows) // 8):
            tile = x_ref[pl.ds(group * rows * 8 + 64 * k + s, 8, stride=8), :]
            first[pl.ds(r * stride + 8 * k - begin, 8), :] = (tile - mean) * gain
        for i in range(lead if ending else 0):
            row = other_ref[pl.ds(2 * ch + (group * lead + i) * 8 + s, 1), :]
            first[pl.ds(r * stride + rows - begin + i, 1), :] = (row - mean[:1]) * (gain[:1] * keep)

    lane = lanes()
    source, target = first, second
    for level in range(plan.local_levels):
        size = 2**level
        final = level == plan.local_levels - 1
        tiles = (end - begin + (up(lead, 8) if ending else 0 if final else 8)) // 8
        jobs = table(delays_ref, level, ch)
        for r, (low, high, delay) in enumerate(jobs):
            base = r // (2 * size) * (2 * size)
            low = (base + low) * stride
            high = (base + size + high) * stride
            for k in range(tiles):
                tile = source[pl.ds(pl.multiple_of(low + 8 * k, 8), 8), :] + shifted_tile(
                    source, high + 8 * k, delay, False, lane
                )
                if not final:
                    target[pl.ds(r * stride + 8 * k, 8), :] = tile
                else:
                    put(plan, outs, 0, r, k + begin // 8, tile)
        source, target = target, source


def put(plan, outs, level, r, k, tile):
    for c, (start, stop) in enumerate(plan.chunks):
        if start <= 8 * k < stop and c in outs:
            outs[c][pl.ds(r * (stop - start) + 8 * k - start, 8), :] = tile
    for i in range(8):
        past = 8 * k + i - plan.rows
        if 0 <= past < plan.ext[level] and 0 in outs:
            at = plan.channels * plan.count(0) + past * plan.channels + r
            outs[0][pl.ds(at, 1), :] = tile[i : i + 1]


def gather_rows(plan, c, level, stride, both, own_ref, own_next, got_ref, got_next):
    ch, n = plan.channels, plan.count(c)
    span = ch * 2**level
    for side, (ref, following) in enumerate(((own_ref, own_next), (got_ref, got_next))):
        for r in range(ch):
            at = (side * ch + r) * stride
            for k in range(n // 8):
                both[pl.ds(at + 8 * k, 8), :] = ref[pl.ds(r * n + 8 * k, 8), :]
            if c == 0:
                for i in range(plan.ext[level]):
                    both[pl.ds(at + n + i, 1), :] = ref[pl.ds(ch * n + i * ch + r, 1), :]
            else:
                m = plan.count(c - 1)
                for k in range(up(span // LANES + 1, 8) // 8):
                    both[pl.ds(at + n + 8 * k, 8), :] = following[pl.ds(r * m + 8 * k, 8), :]


def table(delays_ref, level, count):
    return [tuple(delays_ref[level, i, r] for i in range(3)) for r in range(count)]


def merge_jobs(plan, level, stride, delays_ref):
    ch = plan.channels
    upper = lax.axis_index("freq") // 2**level % 2 == 1
    first, second = jnp.where(upper, ch, 0), jnp.where(upper, 0, ch)
    return [((first + a) * stride, (second + b) * stride, d) for a, b, d in table(delays_ref, level, ch)]


def merged_tile(plan, level, both, job, k, lane):
    low, high, delay = job
    wide = plan.channels * 2**level >= LANES
    return both[pl.ds(pl.multiple_of(low + 8 * k, 8), 8), :] + shifted_tile(
        both, high + 8 * k, delay, wide, lane
    )


def merge_kernel(plan, c, level, stride, *refs):
    if c == 0:
        own_ref, got_ref, delays_ref, _, out_ref, both = refs
        own_next = got_next = None
    else:
        own_ref, own_next, got_ref, got_next, delays_ref, _, out_ref, both = refs
    n = plan.count(c)
    jobs = merge_jobs(plan, level, stride, delays_ref)
    gather_rows(plan, c, level, stride, both, own_ref, own_next, got_ref, got_next)
    lane = lanes()
    rows = n + (up(plan.ext[level + 1], 8) if c == 0 else 0)
    outs = {c: out_ref}
    for r in range(plan.channels):
        for k in range(rows // 8):
            tile = merged_tile(plan, level, both, jobs[r], k, lane)
            put(plan, outs, level + 1, r, k + plan.chunks[c][0] // 8, tile)


def boxcars(begin, count, n, pitch, scale, series, caps_ref, box, lane):
    tiles = n // 8
    together = max(d for d in (1, 2, 4, 8) if d * tiles <= 16 or d == 1)

    def some_rows(step, carry):
        places = [(begin + step * together + i, k) for i in range(together) for k in range(tiles)]
        here = [series[pl.ds(r * pitch + 8 * k, 8), :] for r, k in places]
        after = [series[pl.ds(r * pitch + 8 * k + 1, 8), :] for r, k in places]
        running = here
        best = None
        for offset in range(WMAX):
            if offset:
                running = [
                    total + pltpu.roll(jnp.where(lane >= offset, a, b), LANES - offset, 1)
                    for total, a, b in zip(running, here, after)
                ]
            cap = jnp.broadcast_to(caps_ref[pl.ds(offset, 1), :], (8, LANES))
            factor = scale / math.sqrt(offset + 1)
            value = [jnp.minimum(total * factor, cap) for total in running]
            best = value if best is None else [jnp.maximum(a, b) for a, b in zip(best, value)]
        for (r, k), tile in zip(places, best):
            box[pl.ds((r // 8) * (n * 8) + 64 * k + r % 8, 8, stride=8), :] = tile
        return carry

    lax.fori_loop(0, count // together, some_rows, 0)


def final_kernel(plan, c, stride, *refs):
    level = plan.levels - 1
    ch, n = plan.channels, plan.count(c)
    if c == 0:
        own_ref, got_ref, delays_ref, caps_ref, _, out_ref, head_ref, both, series, box, sem = refs
        own_next = got_next = None
    else:
        (own_ref, own_next, got_ref, got_next, after_ref, delays_ref, caps_ref, _, _, out_ref, head_ref,
         both, series, box, sem) = refs
    jobs = merge_jobs(plan, level, stride, delays_ref)
    gather_rows(plan, c, level, stride, both, own_ref, own_next, got_ref, got_next)
    lane = lanes()
    tiles = n // 8
    scale = 1.0 / math.sqrt(ch * plan.freq_count)
    pitch = n + 8
    for r in range(ch):
        for k in range(tiles + (1 if c == 0 else 0)):
            tile = merged_tile(plan, level, both, jobs[r], k, lane)
            series[pl.ds(r * pitch + 8 * k, 8), :] = tile
            if k == 0:
                head_ref[pl.ds(r, 1), :] = tile[:1]
        if c > 0:
            series[pl.ds(r * pitch + n, 1), :] = after_ref[pl.ds(r, 1), :]

    start = plan.chunks[c][0]
    copies = []
    for group in range(ch // 8):
        boxcars(8 * group, 8, n, pitch, scale, series, caps_ref, box, lane)
        copies.append(pltpu.make_async_copy(
            box.at[pl.ds(group * n * 8, n * 8), :],
            out_ref.at[pl.ds((group * plan.rows + start) * 8, n * 8), :],
            sem.at[group],
        ))
        copies[-1].start()
    for copy in copies:
        copy.wait()


VMEM = pl.BlockSpec(memory_space=pltpu.VMEM)
SMEM = pl.BlockSpec(memory_space=pltpu.SMEM)
ANY = pl.BlockSpec(memory_space=pl.ANY)


def f32(*shape):
    return jax.ShapeDtypeStruct(shape, jnp.float32)


def call(kernel, ins, specs, outs, out_specs, scratch, aliases=None):
    return pl.pallas_call(
        kernel,
        in_specs=specs,
        out_shape=outs,
        out_specs=out_specs,
        scratch_shapes=scratch,
        input_output_aliases=aliases or {},
        cost_estimate=pl.CostEstimate(flops=1, bytes_accessed=1, transcendentals=0),
        compiler_params=pltpu.CompilerParams(vmem_limit_bytes=24 * 2**20),
    )(*ins)


def per_device(plan, spectra, local_delays, merge_delays, widths):
    ch, rows = plan.channels, plan.rows
    chunks = range(len(plan.chunks))
    x = spectra.reshape(ch // 8, 8, rows, LANES).transpose(0, 2, 1, 3).reshape(ch * rows, LANES)
    (msg,) = call(
        functools.partial(stats_kernel, plan), (x,), [VMEM], [f32(2 * ch + ch * plan.lead, LANES)], [VMEM], [],
    )
    other = swap(msg, "tm", 1)
    split = plan.chunks[0][0]
    ins, first = [x, msg, other, local_delays, widths], []
    for begin, end in ((split, rows), (0, split)):
        stride = end - begin + up(plan.lead, 8) + 16
        outs = [f32(plan.message_rows(c, 0), LANES) for c in chunks if begin <= plan.chunks[c][0] < end]
        outs += [] if end == rows else [f32(WMAX, LANES)]
        made = call(
            functools.partial(local_kernel, plan, begin, end, stride), ins, [VMEM] * 5 + [ANY] * (len(ins) - 5),
            outs, [VMEM] * len(outs),
            [pltpu.VMEM((2 * ch, LANES), jnp.float32)] + [pltpu.VMEM((ch * stride, LANES), jnp.float32)] * 2,
        )
        first += made
        ins = [*ins, made[0]]
    caps = first.pop()
    held, got = {}, {}
    for c in chunks:
        held[0, c] = first[c]
        got[0, c] = swap(first[c], "freq", 1)
    last, head, result = caps, None, None
    for level, c in sorted(((level, c) for level in range(plan.levels) for c in chunks), key=turn(plan)):
        if True:
            n = plan.count(c)
            span = ch * 2**level
            ahead = span // LANES + 1
            tail = max((up(plan.ext[level + 1], 8) if c == 0 else 0) + ahead, plan.ext[level], up(ahead, 8))
            stride = up(n + tail, 8)
            both = pltpu.VMEM((2 * ch * stride, LANES), jnp.float32)
            near = [c] if c == 0 else [c, c - 1]
            ins = [group[level, i] for group in (held, got) for i in near]
            specs = [VMEM] * len(ins)
            if level < plan.levels - 1:
                (last,) = call(
                    functools.partial(merge_kernel, plan, c, level, stride), (*ins, merge_delays, last),
                    [*specs, VMEM, ANY], [f32(plan.message_rows(c, level + 1), LANES)], [VMEM], [both],
                )
                held[level + 1, c] = last
                got[level + 1, c] = swap(last, "freq", 2 ** (level + 1))
                continue
            if c > 0:
                ins, specs = [*ins, head], [*specs, VMEM]
            ins, specs = [*ins, merge_delays, caps, last], [*specs, VMEM, VMEM, ANY]
            aliases = {}
            if c > 0:
                aliases = {len(ins): 0}
                ins, specs = [*ins, result], [*specs, ANY]
            result, head = call(
                functools.partial(final_kernel, plan, c, stride), ins, specs,
                [f32(ch * rows, LANES), f32(ch, LANES)], [ANY, VMEM],
                [both, pltpu.VMEM((ch * (n + 8), LANES), jnp.float32),
                 pltpu.VMEM((ch * n, LANES), jnp.float32), pltpu.SemaphoreType.DMA((ch // 8,))], aliases,
            )
            last = head
    return result.reshape(ch // 8, rows, 8, LANES).transpose(0, 2, 1, 3).reshape(ch, rows * LANES)


def solution(mesh):
    placed = (P(("beam", "freq"), "tm"), P(None, None, "freq"), P(None, None, "freq"), P())

    def whole(spectra, local_delays, merge_delays, widths):
        channels = spectra.shape[0] // (mesh.shape["beam"] * mesh.shape["freq"])
        block_len = spectra.shape[1] // mesh.shape["tm"]
        plan = Plan(channels, block_len, mesh.shape["freq"], mesh.shape["tm"])
        return jax.shard_map(
            functools.partial(per_device, plan), mesh=mesh, in_specs=placed,
            out_specs=P(("beam", "freq"), "tm"), check_vma=False,
        )(spectra, local_delays, merge_delays, widths)

    return whole
```

```python
import functools
import math

import jax
import jax.numpy as jnp
from jax import lax
from jax.experimental import pallas as pl
from jax.experimental.pallas import tpu as pltpu
from jax.sharding import PartitionSpec as P

WMAX = 32
LANES = 128
EPSILON = 1e-05
SHARES = (2, 2, 2, 2)
LAST = (2, 2, 2, 1, 1)


def up(value, by):
    return -(-value // by) * by


def swap(value, axis, mask):
    pairs = [(source, source ^ mask) for source in range(lax.axis_size(axis))]
    return lax.ppermute(value, axis, pairs)


def shifted_tile(ref, base, delay, wide, lane):
    if wide:
        base = base + delay // LANES
        delay = delay % LANES
    here = ref[pl.ds(base, 8), :]
    after = ref[pl.ds(base + 1, 8), :]
    return pltpu.roll(jnp.where(lane >= delay, here, after), (LANES - delay) % LANES, 1)


def lanes():
    return lax.broadcasted_iota(jnp.int32, (8, LANES), 1)


STEP, WAIT = 1.5, 0.0


def turn(plan):
    return lambda job: (job[1] + STEP * job[0] + WAIT * (job[0] == plan.levels - 1), job[0])


class Plan:
    def __init__(self, channels, block_len, freq_count, tm_count, shares=SHARES):
        self.channels = channels
        self.rows = block_len // LANES
        self.freq_count = freq_count
        self.tm_count = tm_count
        self.local_levels = channels.bit_length() - 1
        self.levels = freq_count.bit_length() - 1
        tiles = self.rows // 8
        total = sum(shares)
        ends = [tiles - tiles * sum(shares[:i]) // total for i in range(len(shares) + 1)]
        self.chunks = [(8 * ends[i + 1], 8 * ends[i]) for i in range(len(shares))]
        reach = WMAX - 1
        need = [reach]
        for level in reversed(range(self.levels)):
            reach += channels * 2**level
            need.append(reach)
        self.ext = [-(-r // LANES) for r in reversed(need)]
        self.lead = -(-(reach + channels - 1) // LANES)

    def count(self, c):
        return self.chunks[c][1] - self.chunks[c][0]

    def message_rows(self, c, level):
        return self.channels * (self.count(c) + (self.ext[level] if c == 0 else 0))


def stats_kernel(plan, x_ref, msg_ref):
    ch, rows = plan.channels, plan.rows
    for group in range(ch // 8):
        base = group * rows * 8
        parts = [x_ref[pl.ds(base + 8 * i, 8), :] for i in range(8)]
        for i in range(8, rows):
            parts[i % 8] = parts[i % 8] + x_ref[pl.ds(base + 8 * i, 8), :]
        while len(parts) > 1:
            parts = [a + b for a, b in zip(parts[::2], parts[1::2])]
        mean = jnp.sum(parts[0], axis=1, keepdims=True) * (1.0 / (rows * LANES))
        mean = jnp.broadcast_to(mean, (8, LANES))
        parts = [jnp.zeros((8, LANES), jnp.float32) for _ in range(8)]
        for i in range(rows):
            off = x_ref[pl.ds(base + 8 * i, 8), :] - mean
            parts[i % 8] = parts[i % 8] + off * off
        while len(parts) > 1:
            parts = [a + b for a, b in zip(parts[::2], parts[1::2])]
        spread = jnp.sum(parts[0], axis=1, keepdims=True)
        msg_ref[pl.ds(8 * group, 8), :] = mean
        msg_ref[pl.ds(ch + 8 * group, 8), :] = jnp.broadcast_to(spread, (8, LANES))
        for i in range(plan.lead):
            msg_ref[pl.ds(2 * ch + (group * plan.lead + i) * 8, 8), :] = x_ref[pl.ds(base + 8 * i, 8), :]


def local_kernel(plan, begin, end, stride, x_ref, mine_ref, other_ref, delays_ref, widths_ref, *rest):
    ch, rows, lead = plan.channels, plan.rows, plan.lead
    ending = end == rows
    here = [c for c, (start, _) in enumerate(plan.chunks) if begin <= start < end]
    rest = rest if ending else rest[1:]
    outs = dict(zip(here, rest))
    stat, first, second = rest[-3:]
    half = rows * LANES
    if not ending:
        width = lax.broadcasted_iota(jnp.int32, (WMAX, LANES), 0) + 1
        caps = jnp.full((WMAX, LANES), -jnp.inf, jnp.float32)
        for k in range(widths_ref.shape[0]):
            caps = jnp.where(width == widths_ref[k], jnp.inf, caps)
        rest[len(here)][...] = caps
    mean_a, mean_b = mine_ref[pl.ds(0, ch), :], other_ref[pl.ds(0, ch), :]
    gap = mean_a - mean_b
    spread = mine_ref[pl.ds(ch, ch), :] + other_ref[pl.ds(ch, ch), :] + gap * gap * (half / 2.0)
    stat[pl.ds(0, ch), :] = (mean_a + mean_b) * 0.5
    stat[pl.ds(ch, ch), :] = 1.0 / jnp.sqrt(spread * (1.0 / (2 * half)) + EPSILON)
    last = lax.axis_index("tm") == plan.tm_count - 1
    keep = jnp.where(last, 0.0, 1.0).astype(jnp.float32)

    for r in range(ch):
        group, s = r // 8, r % 8
        mean = jnp.broadcast_to(stat[pl.ds(r, 1), :], (8, LANES))
        gain = jnp.broadcast_to(stat[pl.ds(ch + r, 1), :], (8, LANES))
        for k in range(begin // 8, min(end + 8, rows) // 8):
            tile = x_ref[pl.ds(group * rows * 8 + 64 * k + s, 8, stride=8), :]
            first[pl.ds(r * stride + 8 * k - begin, 8), :] = (tile - mean) * gain
        for i in range(lead if ending else 0):
            row = other_ref[pl.ds(2 * ch + (group * lead + i) * 8 + s, 1), :]
            first[pl.ds(r * stride + rows - begin + i, 1), :] = (row - mean[:1]) * (gain[:1] * keep)

    lane = lanes()
    source, target = first, second
    for level in range(plan.local_levels):
        size = 2**level
        final = level == plan.local_levels - 1
        tiles = (end - begin + (up(lead, 8) if ending else 0 if final else 8)) // 8
        jobs = table(delays_ref, level, ch)
        for r, (low, high, delay) in enumerate(jobs):
            base = r // (2 * size) * (2 * size)
            low = (base + low) * stride
            high = (base + size + high) * stride
            for k in range(tiles):
                tile = source[pl.ds(pl.multiple_of(low + 8 * k, 8), 8), :] + shifted_tile(
                    source, high + 8 * k, delay, False, lane
                )
                if not final:
                    target[pl.ds(r * stride + 8 * k, 8), :] = tile
                else:
                    put(plan, outs, 0, r, k + begin // 8, tile)
        source, target = target, source


def put(plan, outs, level, r, k, tile):
    for c, (start, stop) in enumerate(plan.chunks):
        if start <= 8 * k < stop and c in outs:
            outs[c][pl.ds(r * (stop - start) + 8 * k - start, 8), :] = tile
    for i in range(8):
        past = 8 * k + i - plan.rows
        if 0 <= past < plan.ext[level] and 0 in outs:
            at = plan.channels * plan.count(0) + past * plan.channels + r
            outs[0][pl.ds(at, 1), :] = tile[i : i + 1]


def gather_rows(plan, c, level, stride, both, own_ref, own_next, got_ref, got_next):
    ch, n = plan.channels, plan.count(c)
    span = ch * 2**level
    for side, (ref, following) in enumerate(((own_ref, own_next), (got_ref, got_next))):
        for r in range(ch):
            at = (side * ch + r) * stride
            for k in range(n // 8):
                both[pl.ds(at + 8 * k, 8), :] = ref[pl.ds(r * n + 8 * k, 8), :]
            if c == 0:
                for i in range(plan.ext[level]):
                    both[pl.ds(at + n + i, 1), :] = ref[pl.ds(ch * n + i * ch + r, 1), :]
            else:
                m = plan.count(c - 1)
                for k in range(up(span // LANES + 1, 8) // 8):
                    both[pl.ds(at + n + 8 * k, 8), :] = following[pl.ds(r * m + 8 * k, 8), :]


def table(delays_ref, level, count):
    return [tuple(delays_ref[level, i, r] for i in range(3)) for r in range(count)]


def merge_jobs(plan, level, stride, delays_ref):
    ch = plan.channels
    upper = lax.axis_index("freq") // 2**level % 2 == 1
    first, second = jnp.where(upper, ch, 0), jnp.where(upper, 0, ch)
    return [((first + a) * stride, (second + b) * stride, d) for a, b, d in table(delays_ref, level, ch)]


def merged_tile(plan, level, both, job, k, lane):
    low, high, delay = job
    wide = plan.channels * 2**level >= LANES
    return both[pl.ds(pl.multiple_of(low + 8 * k, 8), 8), :] + shifted_tile(
        both, high + 8 * k, delay, wide, lane
    )


def merge_kernel(plan, target, parts, c, level, stride, *refs):
    if c == 0:
        own_ref, got_ref, delays_ref, _, *out_refs, both = refs
        own_next = got_next = None
    else:
        own_ref, own_next, got_ref, got_next, delays_ref, _, *out_refs, both = refs
    n = plan.count(c)
    jobs = merge_jobs(plan, level, stride, delays_ref)
    gather_rows(plan, c, level, stride, both, own_ref, own_next, got_ref, got_next)
    lane = lanes()
    rows = n + (up(plan.ext[level + 1], 8) if c == 0 else 0)
    outs = dict(zip(parts, out_refs))
    for r in range(plan.channels):
        for k in range(rows // 8):
            tile = merged_tile(plan, level, both, jobs[r], k, lane)
            put(target, outs, level + 1, r, k + plan.chunks[c][0] // 8, tile)


def boxcars(begin, count, n, pitch, scale, series, caps_ref, box, lane):
    tiles = n // 8
    together = max(d for d in (1, 2, 4, 8) if d * tiles <= 16 or d == 1)

    def some_rows(step, carry):
        places = [(begin + step * together + i, k) for i in range(together) for k in range(tiles)]
        here = [series[pl.ds(r * pitch + 8 * k, 8), :] for r, k in places]
        after = [series[pl.ds(r * pitch + 8 * k + 1, 8), :] for r, k in places]
        running = here
        best = None
        for offset in range(WMAX):
            if offset:
                running = [
                    total + pltpu.roll(jnp.where(lane >= offset, a, b), LANES - offset, 1)
                    for total, a, b in zip(running, here, after)
                ]
            cap = jnp.broadcast_to(caps_ref[pl.ds(offset, 1), :], (8, LANES))
            factor = scale / math.sqrt(offset + 1)
            value = [jnp.minimum(total * factor, cap) for total in running]
            best = value if best is None else [jnp.maximum(a, b) for a, b in zip(best, value)]
        for (r, k), tile in zip(places, best):
            box[pl.ds((r // 8) * (n * 8) + 64 * k + r % 8, 8, stride=8), :] = tile
        return carry

    lax.fori_loop(0, count // together, some_rows, 0)


def final_kernel(plan, c, stride, *refs):
    level = plan.levels - 1
    ch, n = plan.channels, plan.count(c)
    if c == 0:
        own_ref, got_ref, delays_ref, caps_ref, _, out_ref, head_ref, both, series, box, sem = refs
        own_next = got_next = None
    else:
        (own_ref, own_next, got_ref, got_next, after_ref, delays_ref, caps_ref, _, _, out_ref, head_ref,
         both, series, box, sem) = refs
    jobs = merge_jobs(plan, level, stride, delays_ref)
    gather_rows(plan, c, level, stride, both, own_ref, own_next, got_ref, got_next)
    lane = lanes()
    tiles = n // 8
    scale = 1.0 / math.sqrt(ch * plan.freq_count)
    pitch = n + 8
    for r in range(ch):
        for k in range(tiles + (1 if c == 0 else 0)):
            tile = merged_tile(plan, level, both, jobs[r], k, lane)
            series[pl.ds(r * pitch + 8 * k, 8), :] = tile
            if k == 0:
                head_ref[pl.ds(r, 1), :] = tile[:1]
        if c > 0:
            series[pl.ds(r * pitch + n, 1), :] = after_ref[pl.ds(r, 1), :]

    start = plan.chunks[c][0]
    copies = []
    for group in range(ch // 8):
        boxcars(8 * group, 8, n, pitch, scale, series, caps_ref, box, lane)
        copies.append(pltpu.make_async_copy(
            box.at[pl.ds(group * n * 8, n * 8), :],
            out_ref.at[pl.ds((group * plan.rows + start) * 8, n * 8), :],
            sem.at[group],
        ))
        copies[-1].start()
    for copy in copies:
        copy.wait()


VMEM = pl.BlockSpec(memory_space=pltpu.VMEM)
SMEM = pl.BlockSpec(memory_space=pltpu.SMEM)
ANY = pl.BlockSpec(memory_space=pl.ANY)


def f32(*shape):
    return jax.ShapeDtypeStruct(shape, jnp.float32)


def call(kernel, ins, specs, outs, out_specs, scratch, aliases=None):
    return pl.pallas_call(
        kernel,
        in_specs=specs,
        out_shape=outs,
        out_specs=out_specs,
        scratch_shapes=scratch,
        input_output_aliases=aliases or {},
        cost_estimate=pl.CostEstimate(flops=1, bytes_accessed=1, transcendentals=0),
        compiler_params=pltpu.CompilerParams(vmem_limit_bytes=24 * 2**20),
    )(*ins)


def per_device(plan, fine, spectra, local_delays, merge_delays, widths):
    ch, rows = plan.channels, plan.rows
    chunks = range(len(plan.chunks))
    x = spectra.reshape(ch // 8, 8, rows, LANES).transpose(0, 2, 1, 3).reshape(ch * rows, LANES)
    (msg,) = call(
        functools.partial(stats_kernel, plan), (x,), [VMEM], [f32(2 * ch + ch * plan.lead, LANES)], [VMEM], [],
    )
    other = swap(msg, "tm", 1)
    split = plan.chunks[0][0]
    ins, first = [x, msg, other, local_delays, widths], []
    for begin, end in ((split, rows), (0, split)):
        stride = end - begin + up(plan.lead, 8) + 16
        outs = [f32(plan.message_rows(c, 0), LANES) for c in chunks if begin <= plan.chunks[c][0] < end]
        outs += [] if end == rows else [f32(WMAX, LANES)]
        made = call(
            functools.partial(local_kernel, plan, begin, end, stride), ins, [VMEM] * 5 + [ANY] * (len(ins) - 5),
            outs, [VMEM] * len(outs),
            [pltpu.VMEM((2 * ch, LANES), jnp.float32)] + [pltpu.VMEM((ch * stride, LANES), jnp.float32)] * 2,
        )
        first += made
        ins = [*ins, made[0]]
    caps = first.pop()
    held, got = {}, {}
    for c in chunks:
        held[0, c] = first[c]
        got[0, c] = swap(first[c], "freq", 1)
    last, head, result = caps, None, None
    top = plan.levels - 1
    if any(fine.count(c) < up(ch * 2**top // LANES + 1, 8) for c in range(len(fine.chunks))):
        fine = plan
    jobs = [(level, c) for level in range(top) for c in chunks]
    jobs += [(top, c) for c in range(len(fine.chunks))]
    for level, c in sorted(jobs, key=turn(plan)):
        if True:
            used = fine if level == top else plan
            n = used.count(c)
            span = ch * 2**level
            ahead = span // LANES + 1
            tail = max((up(plan.ext[level + 1], 8) if c == 0 else 0) + ahead, plan.ext[level], up(ahead, 8))
            stride = up(n + tail, 8)
            both = pltpu.VMEM((2 * ch * stride, LANES), jnp.float32)
            near = [c] if c == 0 else [c, c - 1]
            ins = [group[level, i] for group in (held, got) for i in near]
            specs = [VMEM] * len(ins)
            if level < plan.levels - 1:
                target = fine if level + 1 == top else plan
                start, stop = plan.chunks[c]
                parts = [i for i, (a, _) in enumerate(target.chunks) if start <= a < stop]
                made = call(
                    functools.partial(merge_kernel, plan, target, parts, c, level, stride),
                    (*ins, merge_delays, last), [*specs, VMEM, ANY],
                    [f32(target.message_rows(i, level + 1), LANES) for i in parts], [VMEM] * len(parts), [both],
                )
                last = made[0]
                for i, message in zip(parts, made):
                    held[level + 1, i] = message
                    got[level + 1, i] = swap(message, "freq", 2 ** (level + 1))
                continue
            if c > 0:
                ins, specs = [*ins, head], [*specs, VMEM]
            ins, specs = [*ins, merge_delays, caps, last], [*specs, VMEM, VMEM, ANY]
            aliases = {}
            if c > 0:
                aliases = {len(ins): 0}
                ins, specs = [*ins, result], [*specs, ANY]
            result, head = call(
                functools.partial(final_kernel, fine, c, stride), ins, specs,
                [f32(ch * rows, LANES), f32(ch, LANES)], [ANY, VMEM],
                [both, pltpu.VMEM((ch * (n + 8), LANES), jnp.float32),
                 pltpu.VMEM((ch * n, LANES), jnp.float32), pltpu.SemaphoreType.DMA((ch // 8,))], aliases,
            )
            last = head
    return result.reshape(ch // 8, rows, 8, LANES).transpose(0, 2, 1, 3).reshape(ch, rows * LANES)


def solution(mesh):
    placed = (P(("beam", "freq"), "tm"), P(None, None, "freq"), P(None, None, "freq"), P())

    def whole(spectra, local_delays, merge_delays, widths):
        channels = spectra.shape[0] // (mesh.shape["beam"] * mesh.shape["freq"])
        block_len = spectra.shape[1] // mesh.shape["tm"]
        plan = Plan(channels, block_len, mesh.shape["freq"], mesh.shape["tm"])
        fine = Plan(channels, block_len, mesh.shape["freq"], mesh.shape["tm"], LAST)
        return jax.shard_map(
            functools.partial(per_device, plan, fine), mesh=mesh, in_specs=placed,
            out_specs=P(("beam", "freq"), "tm"), check_vma=False,
        )(spectra, local_delays, merge_delays, widths)

    return whole
```
